256 devices in a mesh: gz: 16 (over y_lo, z), gy: 16 (over y_hi, x, core).
Axes of the slice: x: 4, y: 4 (y_hi: 2, y_lo: 2; y = y_hi * 2 + y_lo), z: 8, core: 2. Of those that a mesh axis runs over, the one named last changes fastest.
Arguments:
- velocity: float32 [2, 6, 4096, 4096], P(None, None, 'gy', 'gz'), may hold values from -6 to 6
Outputs:
- spectrum: float32 [2, 6, 4096, 4096], P(None, None, 'gy', 'gz')
The draws below stay inside these ranges and needn't reach their ends.
All inputs are finite; a program needn't handle non-finite values.
Results may differ from the reference program's by a relative error of at most 0.000098.
Values sent between devices are 32-bit elements; how exact they have to be, the bound alone decides.
A program may use at most 64 MiB of HBM per device.

```python
import jax
import jax.numpy as jnp
import numpy as np
from jax import lax

PLANES = 6
NY = 4096
NZ = 4096
N_GZ = 16
N_GY = 16


def level_of(rng, dims, pieces, low, high):
    def one(axis_at, blocks):
        draws = jax.random.uniform(jax.random.fold_in(jax.random.fold_in(rng, 6), axis_at), (blocks,), jnp.float32, low / len(pieces), high / len(pieces))
        return jnp.repeat(jnp.exp(draws), dims[axis_at] // blocks).reshape((-1,) + (1,) * (len(dims) - axis_at - 1))

    gain = one(*pieces[0])
    for cut in pieces[1:]:
        gain = gain * one(*cut)
    return gain


def scatter_about(own_key, extent, scale, bound, cuts=(), kind=jnp.bfloat16):
    drawn = scale * jax.random.normal(own_key, extent, jnp.float32)
    if cuts:
        drawn = drawn * level_of(own_key, extent, cuts, -0.22, 0.18)
    return jnp.clip(drawn, -bound, bound).astype(kind)


def setup_inputs(seed: int = 0) -> dict:
    splits = jax.random.split(jax.random.key(seed), 2)
    velocity = scatter_about(splits[0], (2, PLANES, NY, NZ), 1.0, 6.0, ((2, 16), (3, 16)), jnp.float32)
    return {"velocity": velocity}


def reversed_order(device_count):
    bit_count = device_count.bit_length() - 1
    result = []
    for column in range(device_count):
        value = 0
        for place in range(bit_count):
            value += ((column >> place) & 1) << (bit_count - 1 - place)
        result.append(value)
    return np.array(result, dtype=np.int32)


def reorder_axis(complex_field, axis_number, device_count):
    moved = jnp.moveaxis(complex_field, axis_number, -1)
    length = moved.shape[-1]
    local_len = length // device_count
    split = moved.reshape(moved.shape[:-1] + (local_len, device_count))
    split = jnp.swapaxes(split, -1, -2)
    split = jnp.take(split, jnp.asarray(reversed_order(device_count)), axis=-2)
    placed = split.reshape(moved.shape)
    return jnp.moveaxis(placed, -1, axis_number)


def reference(velocity):
    complex_field = lax.complex(velocity[0], velocity[1])
    transformed = jnp.fft.fft(complex_field, axis=-1, norm="ortho")
    transformed = jnp.fft.fft(transformed, axis=-2, norm="ortho")
    transformed = reorder_axis(transformed, 2, N_GZ)
    transformed = reorder_axis(transformed, 1, N_GY)
    return jnp.stack([jnp.real(transformed), jnp.imag(transformed)]).astype(jnp.float32)
```

```python
import functools

import jax
import jax.numpy as jnp
import ml_dtypes
import numpy as np
from jax import lax
from jax.experimental import pallas as pl
from jax.experimental.pallas import tpu as pltpu
from jax.sharding import PartitionSpec as P

MESH = pl.DeviceIdType.MESH
F32 = jnp.float32
BF16 = jnp.bfloat16
CHUNKS = 3
NZD = 8
NQD = 32


def reversed_bits(value):
    return int(format(value, "04b")[::-1], 2)


def split_host(table):
    high = table.astype(np.float32).astype(ml_dtypes.bfloat16)
    low = (table - high.astype(np.float64)).astype(ml_dtypes.bfloat16)
    return np.stack([high, low])


def device_table():
    index = np.arange(256)
    q, z = index // NZD, index % NZD
    cz, cy = q // 16 * 8 + z, q % 16
    kz = np.array([reversed_bits(c) for c in cz])
    ky = np.array([reversed_bits(c) for c in cy])
    phase = -2.0 * np.pi * ((kz[:, None] * cz[None, :] + ky[:, None] * cy[None, :]) % 16) / 16
    c, s = np.cos(phase), np.sin(phase)
    return split_host(np.block([[c, -s], [s, c]]))


def local_table():
    index = np.arange(256)
    phase = -2.0 * np.pi * ((index[:, None] * index[None, :]) % 256) / 256
    return (np.stack([np.cos(phase), np.sin(phase)]) / 64).astype(np.float32)


def twiddle_table():
    frequency = np.array([reversed_bits(c) for c in range(16)])
    phase = -2.0 * np.pi * ((frequency[:, None] * np.arange(256)[None, :]) % 4096) / 4096
    both = np.stack([np.cos(phase), np.sin(phase)], axis=1).astype(np.float32)
    return np.repeat(both[:, :, None, :], 8, axis=2)


def split(values):
    high = values.astype(BF16)
    return high, (values - high.astype(F32)).astype(BF16)


def mm(left, right):
    return jnp.dot(left, right, preferred_element_type=F32)


def kernel(
    x_hbm, gdev_hbm, floc_hbm, twid_hbm, o_hbm,
    xin, send_p, recv_p, mid_in, mid_out, recv_q, recv_r, out, gdev, floc, twid, ytab, ztab,
    in_sem, const_sem, out_sem, psend, precv, qsend, qrecv, bsend, brecv, rsend, rrecv,
):
    gz, gy = lax.axis_index("gz"), lax.axis_index("gy")
    yl, z = gz // 8, gz % 8
    yh, xc, co = gy // 8, gy // 2 % 4, gy % 2
    yc = yh * 2 + yl
    q = yl * 16 + gy

    def z_partner(t):
        zt = (z + t) % 8
        return zt, (yl * 8 + zt, gy)

    def q_partner(t):
        y2, x2, c2 = (yc + t // 8) % 4, (xc + t // 2 % 4) % 4, (co + t % 2) % 2
        gy2 = y2 // 2 * 8 + x2 * 2 + c2
        return y2 % 2 * 16 + gy2, (y2 % 2 * 8 + z, gy2)

    loads = [pltpu.make_async_copy(x_hbm.at[:, pl.ds(2 * c, 2)], xin.at[:, pl.ds(2 * c, 2)], in_sem.at[c]) for c in range(CHUNKS)]
    for copy in loads:
        copy.start()
    consts = [
        pltpu.make_async_copy(floc_hbm, floc, const_sem.at[0]),
        pltpu.make_async_copy(twid_hbm, twid, const_sem.at[1]),
        pltpu.make_async_copy(gdev_hbm, gdev, const_sem.at[2]),
    ]
    for copy in consts:
        copy.start()

    barrier = pltpu.get_barrier_semaphore()

    @pl.loop(1, 8)
    def _(t):
        pl.semaphore_signal(barrier, inc=1, device_id=z_partner(t)[1], device_id_type=MESH)

    @pl.loop(1, 32)
    def _(t):
        pl.semaphore_signal(barrier, inc=1, device_id=q_partner(t)[1], device_id_type=MESH)

    def relayout(c):
        flat = send_p.at[c].reshape(2048, 128)
        for p in range(2):
            for r in range(2):
                for h in range(2):
                    flat[pl.ds(p * 4 + r * 2 + h, 256, stride=8), :] = xin[r, 2 * c + p, :, h * 128 : h * 128 + 128]

    def p_copy(c, t):
        zt, target = z_partner(t)
        return pltpu.make_async_remote_copy(
            send_p.at[c, pl.ds(zt * 32, 32)], recv_p.at[c, z], psend.at[c, t], precv.at[c, t], device_id=target, device_id_type=MESH
        )

    def p_own(c):
        return pltpu.make_async_copy(send_p.at[c, pl.ds(z * 32, 32)], recv_p.at[c, z], precv.at[c, 0])

    def q_copy(c, t):
        qt, target = q_partner(t)
        return pltpu.make_async_remote_copy(
            recv_p.at[c, :, qt], mid_in.at[c, pl.ds(q * 8, 8)], qsend.at[c, t], qrecv.at[c, t], device_id=target, device_id_type=MESH
        )

    def q_own(c):
        return pltpu.make_async_copy(recv_p.at[c, :, q], mid_in.at[c, pl.ds(q * 8, 8)], qrecv.at[c, 0])

    def b_copy(c, t):
        qt, target = q_partner(t)
        return pltpu.make_async_remote_copy(
            mid_out.at[c, pl.ds(qt * 8, 8)], recv_q.at[c, :, q], bsend.at[c, t], brecv.at[c, t], device_id=target, device_id_type=MESH
        )

    def b_own(c):
        return pltpu.make_async_copy(mid_out.at[c, pl.ds(q * 8, 8)], recv_q.at[c, :, q], brecv.at[c, 0])

    def r_copy(c, t):
        zt, target = z_partner(t)
        return pltpu.make_async_remote_copy(
            recv_q.at[c, zt], recv_r.at[c, pl.ds(z * 32, 32)], rsend.at[c, t], rrecv.at[c, t], device_id=target, device_id_type=MESH
        )

    def r_own(c):
        return pltpu.make_async_copy(recv_q.at[c, z], recv_r.at[c, pl.ds(z * 32, 32)], rrecv.at[c, 0])

    def start(copy, own, count, c):
        own(c).start()

        @pl.loop(1, count)
        def _(t):
            copy(c, t).start()

    def arrived(copy, own, count, c):
        own(c).wait()

        @pl.loop(1, count)
        def _(t):
            copy(c, t).wait_recv()

    def arrived_some(copy, c, low, high):
        @pl.loop(low, high)
        def _(t):
            copy(c, t).wait_recv()

    def sent(copy, count):
        for c in range(CHUNKS):

            @pl.loop(1, count)
            def _(t):
                copy(c, t).wait_send()

    def read_rows(ref):
        flat = ref.reshape(2048, 128)
        rows = [
            jnp.concatenate([flat[pl.ds(p * 4 + r * 2 + h, 256, stride=8), :] for p in range(2) for h in range(2)], axis=1)
            for r in range(2)
        ]
        return jnp.concatenate(rows, axis=0)

    def middle(c):
        xh, xl = split(read_rows(mid_in.at[c]))
        y = mm(gdev[0], xh) + mm(gdev[0], xl) + mm(gdev[1], xh)
        flat = mid_out.at[c].reshape(2048, 128)
        for p in range(2):
            for r in range(2):
                for h in range(2):
                    flat[pl.ds(p * 4 + r * 2 + h, 256, stride=8), :] = y[r * 256 : r * 256 + 256, (p * 2 + h) * 128 : (p * 2 + h) * 128 + 128]

    def tables():
        fr, fi = floc[0], floc[1]

        def twisted(position):
            tc, ts = twid[position, 0, 0:1], twid[position, 1, 0:1]
            return fr * tc - fi * ts, fr * ts + fi * tc

        a, b = twisted(gy)
        full = jnp.concatenate([jnp.concatenate([a, -b], axis=1), jnp.concatenate([b, a], axis=1)], axis=0)
        high, low = split(full)
        ytab[0] = high
        ytab[1] = low
        a, b = twisted(gz)
        a, b = a.T, b.T
        full = jnp.concatenate([jnp.concatenate([a, b], axis=1), jnp.concatenate([-b, a], axis=1)], axis=0)
        high, low = split(full)
        ztab[0] = high
        ztab[1] = low

    def store(c):
        return pltpu.make_async_copy(out.at[:, pl.ds(2 * c, 2)], o_hbm.at[:, pl.ds(2 * c, 2)], out_sem.at[c])

    def final(c):
        xh, xl = split(read_rows(recv_r.at[c]))
        u = mm(ytab[0], xh) + mm(ytab[0], xl) + mm(ytab[1], xh)
        for p in range(2):
            w = jnp.concatenate([u[:256, p * 256 : p * 256 + 256], u[256:, p * 256 : p * 256 + 256]], axis=1)
            wh, wl = split(w)
            v = mm(wh, ztab[0]) + mm(wl, ztab[0]) + mm(wh, ztab[1])
            out[0, 2 * c + p] = v[:, :256]
            out[1, 2 * c + p] = v[:, 256:]
        store(c).start()

    PZ = functools.partial
    loads[0].wait()
    relayout(0)
    pl.semaphore_wait(barrier, 38)
    start(p_copy, p_own, 8, 0)
    loads[1].wait()
    relayout(1)
    loads[2].wait()
    relayout(2)
    for copy in consts:
        copy.wait()
    tables()
    arrived_some(p_copy, 0, 1, 4)
    start(p_copy, p_own, 8, 1)
    p_own(0).wait()
    arrived_some(p_copy, 0, 4, 8)
    start(q_copy, q_own, 32, 0)
    arrived_some(p_copy, 1, 1, 4)
    start(p_copy, p_own, 8, 2)
    arrived(q_copy, q_own, 32, 0)
    middle(0)
    start(b_copy, b_own, 32, 0)
    p_own(1).wait()
    arrived_some(p_copy, 1, 4, 8)
    start(q_copy, q_own, 32, 1)
    arrived(b_copy, b_own, 32, 0)
    arrived_some(p_copy, 2, 1, 4)
    start(r_copy, r_own, 8, 0)
    p_own(2).wait()
    arrived_some(p_copy, 2, 4, 8)
    start(q_copy, q_own, 32, 2)
    arrived(q_copy, q_own, 32, 1)
    middle(1)
    start(b_copy, b_own, 32, 1)
    arrived(b_copy, b_own, 32, 1)
    arrived_some(r_copy, 0, 1, 4)
    start(r_copy, r_own, 8, 1)
    arrived(q_copy, q_own, 32, 2)
    middle(2)
    start(b_copy, b_own, 32, 2)
    r_own(0).wait()
    arrived_some(r_copy, 0, 4, 8)
    final(0)
    arrived(b_copy, b_own, 32, 2)
    arrived_some(r_copy, 1, 1, 4)
    start(r_copy, r_own, 8, 2)
    r_own(1).wait()
    arrived_some(r_copy, 1, 4, 8)
    final(1)
    arrived(r_copy, r_own, 8, 2)
    final(2)
    sent(p_copy, 8)
    sent(q_copy, 32)
    sent(b_copy, 32)
    sent(r_copy, 8)
    for c in range(CHUNKS):
        store(c).wait()


def solution(mesh):
    gdev, floc, twid = device_table(), local_table(), twiddle_table()

    def step(velocity):
        anywhere = pl.BlockSpec(memory_space=pl.ANY)
        tiles = pltpu.VMEM((CHUNKS, 256, 8, 128), F32)
        return pl.pallas_call(
            kernel,
            out_shape=jax.ShapeDtypeStruct(velocity.shape, F32),
            in_specs=[anywhere] * 4,
            out_specs=anywhere,
            scratch_shapes=[
                pltpu.VMEM((2, 6, 256, 256), F32),
                tiles,
                pltpu.VMEM((CHUNKS, 8, 32, 8, 128), F32),
                tiles,
                tiles,
                pltpu.VMEM((CHUNKS, 8, 32, 8, 128), F32),
                tiles,
                pltpu.VMEM((2, 6, 256, 256), F32),
                pltpu.VMEM((2, 512, 512), BF16),
                pltpu.VMEM((2, 256, 256), F32),
                pltpu.VMEM((16, 2, 8, 256), F32),
                pltpu.VMEM((2, 512, 512), BF16),
                pltpu.VMEM((2, 512, 512), BF16),
                pltpu.SemaphoreType.DMA((CHUNKS,)),
                pltpu.SemaphoreType.DMA((3,)),
                pltpu.SemaphoreType.DMA((CHUNKS,)),
                pltpu.SemaphoreType.DMA((CHUNKS, 8)),
                pltpu.SemaphoreType.DMA((CHUNKS, 8)),
                pltpu.SemaphoreType.DMA((CHUNKS, 32)),
                pltpu.SemaphoreType.DMA((CHUNKS, 32)),
                pltpu.SemaphoreType.DMA((CHUNKS, 32)),
                pltpu.SemaphoreType.DMA((CHUNKS, 32)),
                pltpu.SemaphoreType.DMA((CHUNKS, 8)),
                pltpu.SemaphoreType.DMA((CHUNKS, 8)),
            ],
            compiler_params=pltpu.CompilerParams(collective_id=0, has_side_effects=True, vmem_limit_bytes=56 * 2**20),
        )(velocity, jnp.asarray(gdev), jnp.asarray(floc), jnp.asarray(twid))

    return jax.shard_map(
        step, mesh=mesh, in_specs=(P(None, None, "gy", "gz"),), out_specs=P(None, None, "gy", "gz"), check_vma=False
    )
```

```python
import jax
import jax.numpy as jnp
import ml_dtypes
import numpy as np
from jax import lax
from jax.experimental import pallas as pl
from jax.experimental.pallas import tpu as pltpu
from jax.sharding import PartitionSpec as P

MESH = pl.DeviceIdType.MESH
F32 = jnp.float32
BF16 = jnp.bfloat16
CHUNKS = 3
NZD = 8


def reversed_bits(value):
    return int(format(value, "04b")[::-1], 2)


def split_host(table):
    high = table.astype(np.float32).astype(ml_dtypes.bfloat16)
    low = (table - high.astype(np.float64)).astype(ml_dtypes.bfloat16)
    return np.stack([high, low])


def device_table():
    index = np.arange(256)
    q, z = index // NZD, index % NZD
    core, y, x = q // 16, q // 4 % 4, q % 4
    cz, cy = y % 2 * 8 + z, y // 2 * 8 + x * 2 + core
    kz = np.array([reversed_bits(c) for c in cz])
    ky = np.array([reversed_bits(c) for c in cy])
    phase = -2.0 * np.pi * ((kz[:, None] * cz[None, :] + ky[:, None] * cy[None, :]) % 16) / 16
    c, s = np.cos(phase), np.sin(phase)
    return split_host(np.block([[c, -s], [s, c]]))


def local_order():
    half, z, row = np.meshgrid(np.arange(2), np.arange(8), np.arange(16), indexing="ij")
    return (z * 32 + half * 16 + row).reshape(256)


def local_table(order):
    index = np.arange(256)
    phase = -2.0 * np.pi * ((index[:, None] * order[None, :]) % 256) / 256
    return (np.stack([np.cos(phase), np.sin(phase)]) / 64).astype(np.float32)


def twiddle_table(order):
    frequency = np.array([reversed_bits(c) for c in range(16)])
    phase = -2.0 * np.pi * ((frequency[:, None] * order[None, :]) % 4096) / 4096
    both = np.stack([np.cos(phase), np.sin(phase)], axis=1).astype(np.float32)
    return np.repeat(both[:, :, None, :], 8, axis=2)


def split(values):
    high = values.astype(BF16)
    return high, (values - high.astype(F32)).astype(BF16)


def mm(left, right):
    return jnp.dot(left, right, preferred_element_type=F32)


def kernel(
    x_hbm, gdev_hbm, floc_hbm, twid_hbm, o_hbm,
    xin, send_p, recv_p, mid_in, mid_out, recv_q, recv_r, part, out, gdev, floc, twid, ytab, ztab,
    in_sem, const_sem, out_sem, psend, precv, qsend, qrecv, bsend, brecv, rsend, rrecv,
):
    gz, gy = lax.axis_index("gz"), lax.axis_index("gy")
    yl, z = gz // 8, gz % 8
    yh, xc, co = gy // 8, gy // 2 % 4, gy % 2
    yc = yh * 2 + yl
    row = yc * 4 + xc
    q = co * 16 + row

    def z_partner(t):
        zt = (z + t) % 8
        return zt, (yl * 8 + zt, gy)

    def q_partner(t, dc):
        a, b = t // 4, t % 4
        dy, dx = a + co * (b - a), b + co * (a - b)
        y2, x2, c2 = (yc + dy) % 4, (xc + dx) % 4, (co + dc) % 2
        return y2 * 4 + x2, (y2 % 2 * 8 + z, y2 // 2 * 8 + x2 * 2 + c2), (dy * 4 + dx) * 2 + dc

    loads = [pltpu.make_async_copy(x_hbm.at[:, pl.ds(2 * c, 2)], xin.at[:, pl.ds(2 * c, 2)], in_sem.at[c]) for c in range(CHUNKS)]
    consts = [
        pltpu.make_async_copy(floc_hbm, floc, const_sem.at[0]),
        pltpu.make_async_copy(twid_hbm, twid, const_sem.at[1]),
        pltpu.make_async_copy(gdev_hbm, gdev, const_sem.at[2]),
    ]
    for copy in loads + consts:
        copy.start()

    barrier = pltpu.get_barrier_semaphore()

    @pl.loop(1, 8)
    def _(t):
        pl.semaphore_signal(barrier, inc=1, device_id=z_partner(t)[1], device_id_type=MESH)

    @pl.loop(1, 32)
    def _(t):
        pl.semaphore_signal(barrier, inc=1, device_id=q_partner(t // 2, t % 2)[1], device_id_type=MESH)

    def relayout(c, half):
        flat = send_p.at[c, half].reshape(1024, 128)
        for p in range(2):
            for r in range(2):
                for h in range(2):
                    for zt in range(8):
                        first = zt * 32 + half * 16
                        flat[pl.ds(zt * 128 + p * 4 + r * 2 + h, 16, stride=8), :] = xin[r, 2 * c + p, first : first + 16, h * 128 : h * 128 + 128]

    def remote(source, target, send_sem, recv_sem, device):
        return pltpu.make_async_remote_copy(source, target, send_sem, recv_sem, device_id=device, device_id_type=MESH)

    def p_copy(c, half, t):
        zt, device = z_partner(t)
        return remote(send_p.at[c, half, zt], recv_p.at[c, half, z], psend.at[c, half, t], precv.at[c, half, t], device)

    def p_own(c, half):
        return pltpu.make_async_copy(send_p.at[c, half, z], recv_p.at[c, half, z], precv.at[c, half, 0])

    def r_copy(c, half, t):
        zt, device = z_partner(t)
        return remote(recv_q.at[c, half, zt], recv_r.at[c, half, z], rsend.at[c, half, t], rrecv.at[c, half, t], device)

    def r_own(c, half):
        return pltpu.make_async_copy(recv_q.at[c, half, z], recv_r.at[c, half, z], rrecv.at[c, half, 0])

    def q_copy(c, t, dc):
        there, device, slot = q_partner(t, dc)
        half = (co + dc) % 2
        return remote(recv_p.at[c, half, :, there], mid_in.at[c, q], qsend.at[c, slot], qrecv.at[c, slot], device)

    def q_own(c):
        return pltpu.make_async_copy(recv_p.at[c, co, :, row], mid_in.at[c, q], qrecv.at[c, 0])

    def b_copy(c, t, dc):
        there, device, slot = q_partner(t, dc)
        half = (co + dc) % 2
        return remote(mid_out.at[c, half * 16 + there], recv_q.at[c, co, :, row], bsend.at[c, slot], brecv.at[c, slot], device)

    def b_own(c):
        return pltpu.make_async_copy(mid_out.at[c, q], recv_q.at[c, co, :, row], brecv.at[c, 0])

    def start_z(copy, own, c, half):
        own(c, half).start()

        @pl.loop(1, 8)
        def _(t):
            copy(c, half, t).start()

    def wait_z(copy, own, c, half):
        own(c, half).wait()

        @pl.loop(1, 8)
        def _(t):
            copy(c, half, t).wait_recv()

    def start_q(c, half):
        dc = (half + co) % 2

        @pl.loop(1, 8)
        def _(t):
            q_copy(c, t, dc).start()
            q_copy(c, 16 - t, dc).start()

        q_copy(c, 8, dc).start()

        @pl.when(dc == 0)
        def _():
            q_own(c).start()

        @pl.when(dc == 1)
        def _():
            q_copy(c, 0, 1).start()

    def wait_q(c):
        q_own(c).wait()

        @pl.loop(1, 32)
        def _(t):
            q_copy(c, t // 2, t % 2).wait_recv()

    def start_b(c):
        @pl.loop(1, 8)
        def _(t):
            for dc in range(2):
                b_copy(c, t, dc).start()
                b_copy(c, 16 - t, dc).start()

        b_copy(c, 8, 0).start()
        b_copy(c, 8, 1).start()
        b_copy(c, 0, 1).start()
        b_own(c).start()

    def wait_b(c, half):
        dc = (half + co) % 2

        @pl.when(dc == 0)
        def _():
            b_own(c).wait()

        @pl.when(dc == 1)
        def _():
            b_copy(c, 0, 1).wait_recv()

        @pl.loop(1, 16)
        def _(t):
            b_copy(c, t, dc).wait_recv()

    def sent():
        for c in range(CHUNKS):

            @pl.loop(1, 8)
            def _(t):
                for half in range(2):
                    p_copy(c, half, t).wait_send()
                    r_copy(c, half, t).wait_send()

            @pl.loop(1, 32)
            def _(t):
                q_copy(c, t // 2, t % 2).wait_send()
                b_copy(c, t // 2, t % 2).wait_send()

    def read_rows(ref, count):
        flat = ref.reshape(count * 8, 128)
        rows = [
            jnp.concatenate([flat[pl.ds(p * 4 + r * 2 + h, count, stride=8), :] for p in range(2) for h in range(2)], axis=1)
            for r in range(2)
        ]
        return jnp.concatenate(rows, axis=0)

    def middle(c):
        xh, xl = split(read_rows(mid_in.at[c], 256))
        y = mm(gdev[0], xh) + mm(gdev[0], xl) + mm(gdev[1], xh)
        flat = mid_out.at[c].reshape(2048, 128)
        for p in range(2):
            for r in range(2):
                for h in range(2):
                    flat[pl.ds(p * 4 + r * 2 + h, 256, stride=8), :] = y[r * 256 : r * 256 + 256, (p * 2 + h) * 128 : (p * 2 + h) * 128 + 128]

    def twisted(axis, position):
        fr, fi = floc[axis, 0], floc[axis, 1]
        tc, ts = twid[axis, position, 0, 0:1], twid[axis, position, 1, 0:1]
        return fr * tc - fi * ts, fr * ts + fi * tc

    def tables():
        a, b = twisted(0, gy)
        for half in range(2):
            ah, bh = a[:, half * 128 : half * 128 + 128], b[:, half * 128 : half * 128 + 128]
            full = jnp.concatenate([jnp.concatenate([ah, -bh], axis=1), jnp.concatenate([bh, ah], axis=1)], axis=0)
            ytab[half, 0], ytab[half, 1] = split(full)
        a, b = twisted(1, gz)
        a, b = a.T, b.T
        full = jnp.concatenate([jnp.concatenate([a, b], axis=1), jnp.concatenate([-b, a], axis=1)], axis=0)
        ztab[0], ztab[1] = split(full)

    def store(c):
        return pltpu.make_async_copy(out.at[:, pl.ds(2 * c, 2)], o_hbm.at[:, pl.ds(2 * c, 2)], out_sem.at[c])

    def along_y(c, half):
        xh, xl = split(read_rows(recv_r.at[c, half], 128))
        return mm(ytab[half, 0], xh) + mm(ytab[half, 0], xl) + mm(ytab[half, 1], xh)

    def final_first(c):
        part[...] = along_y(c, 0)

    def final_second(c):
        u = part[...] + along_y(c, 1)
        for p in range(2):
            w = jnp.concatenate([u[:256, p * 256 : p * 256 + 256], u[256:, p * 256 : p * 256 + 256]], axis=1)
            wh, wl = split(w)
            v = mm(wh, ztab[0]) + mm(wl, ztab[0]) + mm(wh, ztab[1])
            out[0, 2 * c + p] = v[:, :256]
            out[1, 2 * c + p] = v[:, 256:]
        store(c).start()

    loads[0].wait()
    relayout(0, 0)
    pl.semaphore_wait(barrier, 38)
    start_z(p_copy, p_own, 0, 0)
    relayout(0, 1)
    start_z(p_copy, p_own, 0, 1)
    for c in range(1, CHUNKS):
        loads[c].wait()
        relayout(c, 0)
        relayout(c, 1)
    for copy in consts:
        copy.wait()
    tables()
    wait_z(p_copy, p_own, 0, 0)
    start_q(0, 0)
    start_z(p_copy, p_own, 1, 0)
    wait_z(p_copy, p_own, 0, 1)
    start_q(0, 1)
    start_z(p_copy, p_own, 1, 1)
    wait_q(0)
    middle(0)
    start_b(0)
    wait_z(p_copy, p_own, 1, 0)
    start_q(1, 0)
    start_z(p_copy, p_own, 2, 0)
    wait_z(p_copy, p_own, 1, 1)
    start_q(1, 1)
    start_z(p_copy, p_own, 2, 1)
    wait_b(0, 0)
    start_z(r_copy, r_own, 0, 0)
    wait_b(0, 1)
    start_z(r_copy, r_own, 0, 1)
    wait_q(1)
    middle(1)
    start_b(1)
    wait_z(p_copy, p_own, 2, 0)
    start_q(2, 0)
    wait_z(p_copy, p_own, 2, 1)
    start_q(2, 1)
    wait_b(1, 0)
    start_z(r_copy, r_own, 1, 0)
    wait_b(1, 1)
    start_z(r_copy, r_own, 1, 1)
    wait_q(2)
    middle(2)
    start_b(2)
    wait_z(r_copy, r_own, 0, 0)
    final_first(0)
    wait_z(r_copy, r_own, 0, 1)
    final_second(0)
    wait_b(2, 0)
    start_z(r_copy, r_own, 2, 0)
    wait_b(2, 1)
    start_z(r_copy, r_own, 2, 1)
    wait_z(r_copy, r_own, 1, 0)
    final_first(1)
    wait_z(r_copy, r_own, 1, 1)
    final_second(1)
    wait_z(r_copy, r_own, 2, 0)
    final_first(2)
    wait_z(r_copy, r_own, 2, 1)
    final_second(2)
    sent()
    for c in range(CHUNKS):
        store(c).wait()


def solution(mesh):
    gdev = device_table()
    orders = (local_order(), np.arange(256))
    floc = np.stack([local_table(order) for order in orders])
    twid = np.stack([twiddle_table(order) for order in orders])

    def step(velocity):
        anywhere = pl.BlockSpec(memory_space=pl.ANY)
        halves = pltpu.VMEM((CHUNKS, 2, 8, 16, 8, 128), F32)
        middles = pltpu.VMEM((CHUNKS, 32, 8, 8, 128), F32)
        return pl.pallas_call(
            kernel,
            out_shape=jax.ShapeDtypeStruct(velocity.shape, F32),
            in_specs=[anywhere] * 4,
            out_specs=anywhere,
            scratch_shapes=[
                pltpu.VMEM((2, 6, 256, 256), F32),
                halves,
                halves,
                middles,
                middles,
                halves,
                halves,
                pltpu.VMEM((512, 512), F32),
                pltpu.VMEM((2, 6, 256, 256), F32),
                pltpu.VMEM((2, 512, 512), BF16),
                pltpu.VMEM((2, 2, 256, 256), F32),
                pltpu.VMEM((2, 16, 2, 8, 256), F32),
                pltpu.VMEM((2, 2, 512, 256), BF16),
                pltpu.VMEM((2, 512, 512), BF16),
                pltpu.SemaphoreType.DMA((CHUNKS,)),
                pltpu.SemaphoreType.DMA((3,)),
                pltpu.SemaphoreType.DMA((CHUNKS,)),
                pltpu.SemaphoreType.DMA((CHUNKS, 2, 8)),
                pltpu.SemaphoreType.DMA((CHUNKS, 2, 8)),
                pltpu.SemaphoreType.DMA((CHUNKS, 32)),
                pltpu.SemaphoreType.DMA((CHUNKS, 32)),
                pltpu.SemaphoreType.DMA((CHUNKS, 32)),
                pltpu.SemaphoreType.DMA((CHUNKS, 32)),
                pltpu.SemaphoreType.DMA((CHUNKS, 2, 8)),
                pltpu.SemaphoreType.DMA((CHUNKS, 2, 8)),
            ],
            compiler_params=pltpu.CompilerParams(collective_id=0, has_side_effects=True, vmem_limit_bytes=56 * 2**20),
        )(velocity, jnp.asarray(gdev), jnp.asarray(floc), jnp.asarray(twid))

    return jax.shard_map(
        step, mesh=mesh, in_specs=(P(None, None, "gy", "gz"),), out_specs=P(None, None, "gy", "gz"), check_vma=False
    )
```

```python
import jax
import jax.numpy as jnp
import ml_dtypes
import numpy as np
from jax import lax
from jax.experimental import pallas as pl
from jax.experimental.pallas import tpu as pltpu
from jax.sharding import PartitionSpec as P

MESH = pl.DeviceIdType.MESH
F32 = jnp.float32
BF16 = jnp.bfloat16
CHUNKS = 3
NZD = 8


def reversed_bits(value):
    return int(format(value, "04b")[::-1], 2)


def split_host(table):
    high = table.astype(np.float32).astype(ml_dtypes.bfloat16)
    low = (table - high.astype(np.float64)).astype(ml_dtypes.bfloat16)
    return np.stack([high, low])


def device_table():
    index = np.arange(256)
    q, z = index // NZD, index % NZD
    core, y, x = q // 16, q // 4 % 4, q % 4
    cz, cy = y % 2 * 8 + z, y // 2 * 8 + x * 2 + core
    kz = np.array([reversed_bits(c) for c in cz])
    ky = np.array([reversed_bits(c) for c in cy])
    phase = -2.0 * np.pi * ((kz[:, None] * cz[None, :] + ky[:, None] * cy[None, :]) % 16) / 16
    c, s = np.cos(phase), np.sin(phase)
    return split_host(np.block([[c, -s], [s, c]]))


def local_order():
    half, z, row = np.meshgrid(np.arange(2), np.arange(8), np.arange(16), indexing="ij")
    return (z * 32 + half * 16 + row).reshape(256)


def local_table(order):
    index = np.arange(256)
    phase = -2.0 * np.pi * ((index[:, None] * order[None, :]) % 256) / 256
    return (np.stack([np.cos(phase), np.sin(phase)]) / 64).astype(np.float32)


def twiddle_table(order):
    frequency = np.array([reversed_bits(c) for c in range(16)])
    phase = -2.0 * np.pi * ((frequency[:, None] * order[None, :]) % 4096) / 4096
    both = np.stack([np.cos(phase), np.sin(phase)], axis=1).astype(np.float32)
    return np.repeat(both[:, :, None, :], 8, axis=2)


def split(values):
    high = values.astype(BF16)
    return high, (values - high.astype(F32)).astype(BF16)


def mm(left, right):
    return jnp.dot(left, right, preferred_element_type=F32)


def kernel(
    x_hbm, gdev_hbm, floc_hbm, twid_hbm, out,
    xin, send_p, recv_p, mid_in, mid_out, recv_q, recv_r, part, gdev, floc, twid, ytab, ztab,
    in_sem, const_sem, psend, precv, qsend, qrecv, bsend, brecv, rsend, rrecv,
):
    gz, gy = lax.axis_index("gz"), lax.axis_index("gy")
    yl, z = gz // 8, gz % 8
    yh, xc, co = gy // 8, gy // 2 % 4, gy % 2
    yc = yh * 2 + yl
    row = yc * 4 + xc
    q = co * 16 + row

    def z_partner(t):
        zt = (z + t) % 8
        return zt, (yl * 8 + zt, gy)

    def q_partner(t, dc):
        a, b = t // 4, t % 4
        dy, dx = a + co * (b - a), b + co * (a - b)
        y2, x2, c2 = (yc + dy) % 4, (xc + dx) % 4, (co + dc) % 2
        return y2 * 4 + x2, (y2 % 2 * 8 + z, y2 // 2 * 8 + x2 * 2 + c2), (dy * 4 + dx) * 2 + dc

    loads = [pltpu.make_async_copy(x_hbm.at[:, pl.ds(2 * c, 2)], xin.at[:, pl.ds(2 * c, 2)], in_sem.at[c]) for c in range(CHUNKS)]
    consts = [
        pltpu.make_async_copy(floc_hbm, floc, const_sem.at[0]),
        pltpu.make_async_copy(twid_hbm, twid, const_sem.at[1]),
        pltpu.make_async_copy(gdev_hbm, gdev, const_sem.at[2]),
    ]
    for copy in loads + consts:
        copy.start()

    barrier = pltpu.get_barrier_semaphore()

    @pl.loop(1, 8)
    def _(t):
        pl.semaphore_signal(barrier, inc=1, device_id=z_partner(t)[1], device_id_type=MESH)

    @pl.loop(1, 32)
    def _(t):
        pl.semaphore_signal(barrier, inc=1, device_id=q_partner(t // 2, t % 2)[1], device_id_type=MESH)

    def relayout(c, half):
        flat = send_p.at[c, half].reshape(1024, 128)
        for p in range(2):
            for r in range(2):
                for h in range(2):
                    for zt in range(8):
                        first = zt * 32 + half * 16
                        flat[pl.ds(zt * 128 + p * 4 + r * 2 + h, 16, stride=8), :] = xin[r, 2 * c + p, first : first + 16, h * 128 : h * 128 + 128]

    def remote(source, target, send_sem, recv_sem, device):
        return pltpu.make_async_remote_copy(source, target, send_sem, recv_sem, device_id=device, device_id_type=MESH)

    def p_copy(c, half, t):
        zt, device = z_partner(t)
        return remote(send_p.at[c, half, zt], recv_p.at[c, half, z], psend.at[c, half, t], precv.at[c, half, t], device)

    def p_own(c, half):
        return pltpu.make_async_copy(send_p.at[c, half, z], recv_p.at[c, half, z], precv.at[c, half, 0])

    def r_copy(c, half, t):
        zt, device = z_partner(t)
        return remote(recv_q.at[c, half, zt], recv_r.at[c, half, z], rsend.at[c, half, t], rrecv.at[c, half, t], device)

    def r_own(c, half):
        return pltpu.make_async_copy(recv_q.at[c, half, z], recv_r.at[c, half, z], rrecv.at[c, half, 0])

    def q_copy(c, t, dc):
        there, device, slot = q_partner(t, dc)
        half = (co + dc) % 2
        return remote(recv_p.at[c, half, :, there], mid_in.at[c, q], qsend.at[c, slot], qrecv.at[c, slot], device)

    def q_own(c):
        return pltpu.make_async_copy(recv_p.at[c, co, :, row], mid_in.at[c, q], qrecv.at[c, 0])

    def b_copy(c, t, dc):
        there, device, slot = q_partner(t, dc)
        half = (co + dc) % 2
        return remote(mid_out.at[c, half * 16 + there], recv_q.at[c, co, :, row], bsend.at[c, slot], brecv.at[c, slot], device)

    def b_own(c):
        return pltpu.make_async_copy(mid_out.at[c, q], recv_q.at[c, co, :, row], brecv.at[c, 0])

    def start_z(copy, own, c, half):
        own(c, half).start()

        @pl.loop(1, 8)
        def _(t):
            copy(c, half, t).start()

    def wait_z(copy, own, c, half):
        own(c, half).wait()

        @pl.loop(1, 8)
        def _(t):
            copy(c, half, t).wait_recv()

    def start_q(c, half):
        dc = (half + co) % 2

        @pl.loop(1, 8)
        def _(t):
            q_copy(c, t, dc).start()
            q_copy(c, 16 - t, dc).start()

        q_copy(c, 8, dc).start()

        @pl.when(dc == 0)
        def _():
            q_own(c).start()

        @pl.when(dc == 1)
        def _():
            q_copy(c, 0, 1).start()

    def wait_q(c):
        q_own(c).wait()

        @pl.loop(1, 32)
        def _(t):
            q_copy(c, t // 2, t % 2).wait_recv()

    def start_b(c):
        @pl.loop(1, 8)
        def _(t):
            for dc in range(2):
                b_copy(c, t, dc).start()
                b_copy(c, 16 - t, dc).start()

        b_copy(c, 8, 0).start()
        b_copy(c, 8, 1).start()
        b_copy(c, 0, 1).start()
        b_own(c).start()

    def wait_b(c, half):
        dc = (half + co) % 2

        @pl.when(dc == 0)
        def _():
            b_own(c).wait()

        @pl.when(dc == 1)
        def _():
            b_copy(c, 0, 1).wait_recv()

        @pl.loop(1, 16)
        def _(t):
            b_copy(c, t, dc).wait_recv()

    def sent_z(copy, c):
        @pl.loop(1, 8)
        def _(t):
            for half in range(2):
                copy(c, half, t).wait_send()

    def sent_q(copy, c):
        @pl.loop(1, 32)
        def _(t):
            copy(c, t // 2, t % 2).wait_send()

    def read_rows(ref, count):
        flat = ref.reshape(count * 8, 128)
        rows = [
            jnp.concatenate([flat[pl.ds(p * 4 + r * 2 + h, count, stride=8), :] for p in range(2) for h in range(2)], axis=1)
            for r in range(2)
        ]
        return jnp.concatenate(rows, axis=0)

    def middle(c):
        xh, xl = split(read_rows(mid_in.at[c], 256))
        y = mm(gdev[0], xh) + mm(gdev[0], xl) + mm(gdev[1], xh)
        flat = mid_out.at[c].reshape(2048, 128)
        for p in range(2):
            for r in range(2):
                for h in range(2):
                    flat[pl.ds(p * 4 + r * 2 + h, 256, stride=8), :] = y[r * 256 : r * 256 + 256, (p * 2 + h) * 128 : (p * 2 + h) * 128 + 128]

    def twisted(axis, position):
        fr, fi = floc[axis, 0], floc[axis, 1]
        tc, ts = twid[axis, position, 0, 0:1], twid[axis, position, 1, 0:1]
        return fr * tc - fi * ts, fr * ts + fi * tc

    def tables():
        a, b = twisted(0, gy)
        for half in range(2):
            ah, bh = a[:, half * 128 : half * 128 + 128], b[:, half * 128 : half * 128 + 128]
            full = jnp.concatenate([jnp.concatenate([ah, -bh], axis=1), jnp.concatenate([bh, ah], axis=1)], axis=0)
            ytab[half, 0], ytab[half, 1] = split(full)
        a, b = twisted(1, gz)
        a, b = a.T, b.T
        full = jnp.concatenate([jnp.concatenate([a, b], axis=1), jnp.concatenate([-b, a], axis=1)], axis=0)
        ztab[0], ztab[1] = split(full)

    def along_y(c, half):
        xh, xl = split(read_rows(recv_r.at[c, half], 128))
        return mm(ytab[half, 0], xh) + mm(ytab[half, 0], xl) + mm(ytab[half, 1], xh)

    def final_first(c):
        part[...] = along_y(c, 0)

    def final_second(c):
        u = part[...] + along_y(c, 1)
        for p in range(2):
            w = jnp.concatenate([u[:256, p * 256 : p * 256 + 256], u[256:, p * 256 : p * 256 + 256]], axis=1)
            wh, wl = split(w)
            v = mm(wh, ztab[0]) + mm(wl, ztab[0]) + mm(wh, ztab[1])
            out[0, 2 * c + p] = v[:, :256]
            out[1, 2 * c + p] = v[:, 256:]

    loads[0].wait()
    relayout(0, 0)
    pl.semaphore_wait(barrier, 38)
    start_z(p_copy, p_own, 0, 0)
    relayout(0, 1)
    start_z(p_copy, p_own, 0, 1)
    for c in range(1, CHUNKS):
        loads[c].wait()
        relayout(c, 0)
        relayout(c, 1)
    for copy in consts:
        copy.wait()
    tables()
    wait_z(p_copy, p_own, 0, 0)
    start_q(0, 0)
    start_z(p_copy, p_own, 1, 0)
    wait_z(p_copy, p_own, 0, 1)
    start_q(0, 1)
    start_z(p_copy, p_own, 1, 1)
    wait_q(0)
    middle(0)
    start_b(0)
    wait_z(p_copy, p_own, 1, 0)
    start_q(1, 0)
    start_z(p_copy, p_own, 2, 0)
    wait_z(p_copy, p_own, 1, 1)
    start_q(1, 1)
    start_z(p_copy, p_own, 2, 1)
    wait_b(0, 0)
    start_z(r_copy, r_own, 0, 0)
    wait_b(0, 1)
    start_z(r_copy, r_own, 0, 1)
    wait_q(1)
    middle(1)
    start_b(1)
    wait_z(p_copy, p_own, 2, 0)
    start_q(2, 0)
    wait_z(p_copy, p_own, 2, 1)
    start_q(2, 1)
    wait_b(1, 0)
    start_z(r_copy, r_own, 1, 0)
    wait_b(1, 1)
    start_z(r_copy, r_own, 1, 1)
    wait_q(2)
    middle(2)
    start_b(2)
    wait_z(r_copy, r_own, 0, 0)
    final_first(0)
    wait_z(r_copy, r_own, 0, 1)
    final_second(0)
    wait_b(2, 0)
    start_z(r_copy, r_own, 2, 0)
    wait_b(2, 1)
    start_z(r_copy, r_own, 2, 1)
    for c in range(CHUNKS):
        sent_z(p_copy, c)
        sent_q(q_copy, c)
    wait_z(r_copy, r_own, 1, 0)
    final_first(1)
    for c in range(CHUNKS):
        sent_q(b_copy, c)
    wait_z(r_copy, r_own, 1, 1)
    final_second(1)
    sent_z(r_copy, 0)
    sent_z(r_copy, 1)
    wait_z(r_copy, r_own, 2, 0)
    final_first(2)
    wait_z(r_copy, r_own, 2, 1)
    final_second(2)
    sent_z(r_copy, 2)


def solution(mesh):
    gdev = device_table()
    orders = (local_order(), np.arange(256))
    floc = np.stack([local_table(order) for order in orders])
    twid = np.stack([twiddle_table(order) for order in orders])

    def step(velocity):
        anywhere = pl.BlockSpec(memory_space=pl.ANY)
        halves = pltpu.VMEM((CHUNKS, 2, 8, 16, 8, 128), F32)
        middles = pltpu.VMEM((CHUNKS, 32, 8, 8, 128), F32)
        return pl.pallas_call(
            kernel,
            out_shape=pltpu.VMEM(velocity.shape, F32),
            in_specs=[pl.BlockSpec(memory_space=pltpu.HBM)] * 4,
            out_specs=pl.BlockSpec(memory_space=pltpu.VMEM),
            scratch_shapes=[
                pltpu.VMEM((2, 6, 256, 256), F32),
                halves,
                halves,
                middles,
                middles,
                halves,
                halves,
                pltpu.VMEM((512, 512), F32),
                pltpu.VMEM((2, 512, 512), BF16),
                pltpu.VMEM((2, 2, 256, 256), F32),
                pltpu.VMEM((2, 16, 2, 8, 256), F32),
                pltpu.VMEM((2, 2, 512, 256), BF16),
                pltpu.VMEM((2, 512, 512), BF16),
                pltpu.SemaphoreType.DMA((CHUNKS,)),
                pltpu.SemaphoreType.DMA((3,)),
                pltpu.SemaphoreType.DMA((CHUNKS, 2, 8)),
                pltpu.SemaphoreType.DMA((CHUNKS, 2, 8)),
                pltpu.SemaphoreType.DMA((CHUNKS, 32)),
                pltpu.SemaphoreType.DMA((CHUNKS, 32)),
                pltpu.SemaphoreType.DMA((CHUNKS, 32)),
                pltpu.SemaphoreType.DMA((CHUNKS, 32)),
                pltpu.SemaphoreType.DMA((CHUNKS, 2, 8)),
                pltpu.SemaphoreType.DMA((CHUNKS, 2, 8)),
            ],
            compiler_params=pltpu.CompilerParams(collective_id=0, has_side_effects=True, vmem_limit_bytes=40 * 2**20),
        )(*[pltpu.with_memory_space_constraint(a, pltpu.HBM) for a in (velocity, jnp.asarray(gdev), jnp.asarray(floc), jnp.asarray(twid))])

    return jax.shard_map(
        step, mesh=mesh, in_specs=(P(None, None, "gy", "gz"),), out_specs=P(None, None, "gy", "gz"), check_vma=False
    )
```

```python
import jax
import jax.numpy as jnp
import ml_dtypes
import numpy as np
from jax import lax
from jax.experimental import pallas as pl
from jax.experimental.pallas import tpu as pltpu
from jax.sharding import PartitionSpec as P

MESH = pl.DeviceIdType.MESH
F32 = jnp.float32
BF16 = jnp.bfloat16
CHUNKS = 3
NZD = 8


def reversed_bits(value):
    return int(format(value, "04b")[::-1], 2)


def split_host(table):
    high = table.astype(np.float32).astype(ml_dtypes.bfloat16)
    low = (table - high.astype(np.float64)).astype(ml_dtypes.bfloat16)
    return np.stack([high, low])


def device_table():
    index = np.arange(256)
    q, z = index // NZD, index % NZD
    core, y, x = q // 16, q // 4 % 4, q % 4
    cz, cy = y % 2 * 8 + z, y // 2 * 8 + x * 2 + core
    kz = np.array([reversed_bits(c) for c in cz])
    ky = np.array([reversed_bits(c) for c in cy])
    phase = -2.0 * np.pi * ((kz[:, None] * cz[None, :] + ky[:, None] * cy[None, :]) % 16) / 16
    c, s = np.cos(phase), np.sin(phase)
    return split_host(np.block([[c, -s], [s, c]]))


def local_order():
    half, z, row = np.meshgrid(np.arange(2), np.arange(8), np.arange(16), indexing="ij")
    return (z * 32 + half * 16 + row).reshape(256)


def local_table(order):
    index = np.arange(256)
    phase = -2.0 * np.pi * ((index[:, None] * order[None, :]) % 256) / 256
    return (np.stack([np.cos(phase), np.sin(phase)]) / 64).astype(np.float32)


def twiddle_table(order):
    frequency = np.array([reversed_bits(c) for c in range(16)])
    phase = -2.0 * np.pi * ((frequency[:, None] * order[None, :]) % 4096) / 4096
    both = np.stack([np.cos(phase), np.sin(phase)], axis=1).astype(np.float32)
    return np.repeat(both[:, :, None, :], 8, axis=2)


def split(values):
    high = values.astype(BF16)
    return high, (values - high.astype(F32)).astype(BF16)


def mm(left, right):
    return jnp.dot(left, right, preferred_element_type=F32)


def kernel(
    x_hbm, gdev_hbm, floc_hbm, twid_hbm, out,
    xin, send_p, recv_p, mid_in, mid_out, recv_q, recv_r, part, gdev, floc, twid, ytab, ztab,
    in_sem, const_sem, psend, precv, qsend, qrecv, bsend, brecv, rsend, rrecv,
):
    gz, gy = lax.axis_index("gz"), lax.axis_index("gy")
    yl, z = gz // 8, gz % 8
    yh, xc, co = gy // 8, gy // 2 % 4, gy % 2
    yc = yh * 2 + yl
    row = yc * 4 + xc
    q = co * 16 + row

    def z_partner(t):
        zt = (z + t) % 8
        return zt, (yl * 8 + zt, gy)

    def q_partner(t, dc):
        a, b = t // 4, t % 4
        dy, dx = a + co * (b - a), b + co * (a - b)
        y2, x2, c2 = (yc + dy) % 4, (xc + dx) % 4, (co + dc) % 2
        return y2 * 4 + x2, (y2 % 2 * 8 + z, y2 // 2 * 8 + x2 * 2 + c2)

    loads = [pltpu.make_async_copy(x_hbm.at[:, pl.ds(2 * c, 2)], xin.at[:, pl.ds(2 * c, 2)], in_sem.at[c]) for c in range(CHUNKS)]
    consts = [
        pltpu.make_async_copy(floc_hbm, floc, const_sem.at[0]),
        pltpu.make_async_copy(twid_hbm, twid, const_sem.at[1]),
        pltpu.make_async_copy(gdev_hbm, gdev, const_sem.at[2]),
    ]
    for copy in loads + consts:
        copy.start()

    barrier = pltpu.get_barrier_semaphore()

    @pl.loop(1, 8)
    def _(t):
        pl.semaphore_signal(barrier, inc=1, device_id=z_partner(t)[1], device_id_type=MESH)

    @pl.loop(1, 32)
    def _(t):
        pl.semaphore_signal(barrier, inc=1, device_id=q_partner(t // 2, t % 2)[1], device_id_type=MESH)

    def relayout(c, half):
        flat = send_p.at[c, half].reshape(1024, 128)
        for p in range(2):
            for r in range(2):
                for h in range(2):
                    for zt in range(8):
                        first = zt * 32 + half * 16
                        flat[pl.ds(zt * 128 + p * 4 + r * 2 + h, 16, stride=8), :] = xin[r, 2 * c + p, first : first + 16, h * 128 : h * 128 + 128]

    def remote(source, target, send_sem, recv_sem, device):
        return pltpu.make_async_remote_copy(source, target, send_sem, recv_sem, device_id=device, device_id_type=MESH)

    def p_copy(c, half, t):
        zt, device = z_partner(t)
        return remote(send_p.at[c, half, zt], recv_p.at[c, half, z], psend.at[c], precv.at[c, half], device)

    def p_own(c, half):
        return pltpu.make_async_copy(send_p.at[c, half, z], recv_p.at[c, half, z], precv.at[c, half])

    def r_copy(c, half, t):
        zt, device = z_partner(t)
        return remote(recv_q.at[c, half, zt], recv_r.at[c, half, z], rsend.at[c], rrecv.at[c, half], device)

    def r_own(c, half):
        return pltpu.make_async_copy(recv_q.at[c, half, z], recv_r.at[c, half, z], rrecv.at[c, half])

    def q_copy(c, t, dc):
        there, device = q_partner(t, dc)
        half = (co + dc) % 2
        return remote(recv_p.at[c, half, :, there], mid_in.at[c, q], qsend.at[c], qrecv.at[c], device)

    def q_own(c):
        return pltpu.make_async_copy(recv_p.at[c, co, :, row], mid_in.at[c, q], qrecv.at[c])

    def b_copy(c, t, dc):
        there, device = q_partner(t, dc)
        half = (co + dc) % 2
        return remote(mid_out.at[c, half * 16 + there], recv_q.at[c, co, :, row], bsend.at[c], brecv.at[c, co], device)

    def b_own(c):
        return pltpu.make_async_copy(mid_out.at[c, q], recv_q.at[c, co, :, row], brecv.at[c, co])

    def start_z(copy, own, c, half):
        own(c, half).start()

        @pl.loop(1, 8)
        def _(t):
            copy(c, half, t).start()

    def wait_bytes(ref, sem):
        pltpu.make_async_copy(ref, ref, sem).wait()

    def start_q(c, half):
        dc = (half + co) % 2

        @pl.loop(1, 8)
        def _(t):
            q_copy(c, t, dc).start()
            q_copy(c, 16 - t, dc).start()

        q_copy(c, 8, dc).start()

        @pl.when(dc == 0)
        def _():
            q_own(c).start()

        @pl.when(dc == 1)
        def _():
            q_copy(c, 0, 1).start()

    def start_b(c):
        @pl.loop(1, 8)
        def _(t):
            for dc in range(2):
                b_copy(c, t, dc).start()
                b_copy(c, 16 - t, dc).start()

        b_copy(c, 8, 0).start()
        b_copy(c, 8, 1).start()
        b_copy(c, 0, 1).start()
        b_own(c).start()

    def read_rows(ref, count):
        flat = ref.reshape(count * 8, 128)
        rows = [
            jnp.concatenate([flat[pl.ds(p * 4 + r * 2 + h, count, stride=8), :] for p in range(2) for h in range(2)], axis=1)
            for r in range(2)
        ]
        return jnp.concatenate(rows, axis=0)

    def middle(c):
        xh, xl = split(read_rows(mid_in.at[c], 256))
        y = mm(gdev[0], xh) + mm(gdev[0], xl) + mm(gdev[1], xh)
        flat = mid_out.at[c].reshape(2048, 128)
        for p in range(2):
            for r in range(2):
                for h in range(2):
                    flat[pl.ds(p * 4 + r * 2 + h, 256, stride=8), :] = y[r * 256 : r * 256 + 256, (p * 2 + h) * 128 : (p * 2 + h) * 128 + 128]

    def twisted(axis, position):
        fr, fi = floc[axis, 0], floc[axis, 1]
        tc, ts = twid[axis, position, 0, 0:1], twid[axis, position, 1, 0:1]
        return fr * tc - fi * ts, fr * ts + fi * tc

    def tables():
        a, b = twisted(0, gy)
        for half in range(2):
            ah, bh = a[:, half * 128 : half * 128 + 128], b[:, half * 128 : half * 128 + 128]
            full = jnp.concatenate([jnp.concatenate([ah, -bh], axis=1), jnp.concatenate([bh, ah], axis=1)], axis=0)
            ytab[half, 0], ytab[half, 1] = split(full)
        a, b = twisted(1, gz)
        a, b = a.T, b.T
        full = jnp.concatenate([jnp.concatenate([a, b], axis=1), jnp.concatenate([-b, a], axis=1)], axis=0)
        ztab[0], ztab[1] = split(full)

    def transformed(c, half):
        flat = recv_r.at[c, half].reshape(1024, 128)
        rows = [jnp.concatenate([flat[pl.ds(p * 4 + s, 128, stride=8), :] for s in range(4)], axis=1) for p in range(2)]
        xh, xl = split(jnp.concatenate(rows, axis=0))
        v = mm(xh, ztab[0]) + mm(xl, ztab[0]) + mm(xh, ztab[1])
        planes = [jnp.concatenate([v[p * 128 : p * 128 + 128, :256], v[p * 128 : p * 128 + 128, 256:]], axis=0) for p in range(2)]
        vh, vl = split(jnp.concatenate(planes, axis=1))
        return mm(ytab[half, 0], vh) + mm(ytab[half, 0], vl) + mm(ytab[half, 1], vh)

    def final_first(c):
        part[...] = transformed(c, 0)

    def final_second(c):
        u = part[...] + transformed(c, 1)
        for p in range(2):
            for r in range(2):
                out[r, 2 * c + p] = u[r * 256 : r * 256 + 256, p * 256 : p * 256 + 256]

    loads[0].wait()
    relayout(0, 0)
    pl.semaphore_wait(barrier, 38)
    start_z(p_copy, p_own, 0, 0)
    relayout(0, 1)
    start_z(p_copy, p_own, 0, 1)
    for c in range(1, CHUNKS):
        loads[c].wait()
        relayout(c, 0)
        relayout(c, 1)
    for copy in consts:
        copy.wait()
    tables()
    wait_bytes(recv_p.at[0, 0], precv.at[0, 0])
    start_q(0, 0)
    start_z(p_copy, p_own, 1, 0)
    wait_bytes(recv_p.at[0, 1], precv.at[0, 1])
    start_q(0, 1)
    start_z(p_copy, p_own, 1, 1)
    wait_bytes(mid_in.at[0], qrecv.at[0])
    middle(0)
    start_b(0)
    wait_bytes(recv_p.at[1, 0], precv.at[1, 0])
    start_q(1, 0)
    start_z(p_copy, p_own, 2, 0)
    wait_bytes(recv_p.at[1, 1], precv.at[1, 1])
    start_q(1, 1)
    start_z(p_copy, p_own, 2, 1)
    wait_bytes(recv_q.at[0, 0], brecv.at[0, 0])
    start_z(r_copy, r_own, 0, 0)
    wait_bytes(recv_q.at[0, 1], brecv.at[0, 1])
    start_z(r_copy, r_own, 0, 1)
    wait_bytes(mid_in.at[1], qrecv.at[1])
    middle(1)
    start_b(1)
    wait_bytes(recv_p.at[2, 0], precv.at[2, 0])
    start_q(2, 0)
    wait_bytes(recv_p.at[2, 1], precv.at[2, 1])
    start_q(2, 1)
    wait_bytes(recv_q.at[1, 0], brecv.at[1, 0])
    start_z(r_copy, r_own, 1, 0)
    wait_bytes(recv_q.at[1, 1], brecv.at[1, 1])
    start_z(r_copy, r_own, 1, 1)
    wait_bytes(mid_in.at[2], qrecv.at[2])
    middle(2)
    start_b(2)
    wait_bytes(recv_r.at[0, 0], rrecv.at[0, 0])
    final_first(0)
    wait_bytes(recv_r.at[0, 1], rrecv.at[0, 1])
    final_second(0)
    wait_bytes(recv_q.at[2, 0], brecv.at[2, 0])
    start_z(r_copy, r_own, 2, 0)
    wait_bytes(recv_q.at[2, 1], brecv.at[2, 1])
    start_z(r_copy, r_own, 2, 1)
    for c in range(CHUNKS):
        wait_bytes(send_p.at[c, :, pl.ds(0, 7)], psend.at[c])
        wait_bytes(mid_in.at[c, pl.ds(0, 31)], qsend.at[c])
    wait_bytes(recv_r.at[1, 0], rrecv.at[1, 0])
    final_first(1)
    for c in range(CHUNKS):
        wait_bytes(mid_out.at[c, pl.ds(0, 31)], bsend.at[c])
    wait_bytes(recv_r.at[1, 1], rrecv.at[1, 1])
    final_second(1)
    wait_bytes(recv_r.at[0, :, pl.ds(0, 7)], rsend.at[0])
    wait_bytes(recv_r.at[1, :, pl.ds(0, 7)], rsend.at[1])
    wait_bytes(recv_r.at[2, 0], rrecv.at[2, 0])
    final_first(2)
    wait_bytes(recv_r.at[2, 1], rrecv.at[2, 1])
    final_second(2)
    wait_bytes(recv_r.at[2, :, pl.ds(0, 7)], rsend.at[2])


def solution(mesh):
    gdev = device_table()
    orders = (local_order(), np.arange(256))
    floc = np.stack([local_table(order) for order in orders])
    twid = np.stack([twiddle_table(order) for order in orders])

    def step(velocity):
        anywhere = pl.BlockSpec(memory_space=pl.ANY)
        halves = pltpu.VMEM((CHUNKS, 2, 8, 16, 8, 128), F32)
        middles = pltpu.VMEM((CHUNKS, 32, 8, 8, 128), F32)
        return pl.pallas_call(
            kernel,
            out_shape=pltpu.VMEM(velocity.shape, F32),
            in_specs=[pl.BlockSpec(memory_space=pltpu.HBM)] * 4,
            out_specs=pl.BlockSpec(memory_space=pltpu.VMEM),
            scratch_shapes=[
                pltpu.VMEM((2, 6, 256, 256), F32),
                halves,
                halves,
                middles,
                middles,
                halves,
                halves,
                pltpu.VMEM((512, 512), F32),
                pltpu.VMEM((2, 512, 512), BF16),
                pltpu.VMEM((2, 2, 256, 256), F32),
                pltpu.VMEM((2, 16, 2, 8, 256), F32),
                pltpu.VMEM((2, 2, 512, 256), BF16),
                pltpu.VMEM((2, 512, 512), BF16),
                pltpu.SemaphoreType.DMA((CHUNKS,)),
                pltpu.SemaphoreType.DMA((3,)),
                pltpu.SemaphoreType.DMA((CHUNKS,)),
                pltpu.SemaphoreType.DMA((CHUNKS, 2)),
                pltpu.SemaphoreType.DMA((CHUNKS,)),
                pltpu.SemaphoreType.DMA((CHUNKS,)),
                pltpu.SemaphoreType.DMA((CHUNKS,)),
                pltpu.SemaphoreType.DMA((CHUNKS, 2)),
                pltpu.SemaphoreType.DMA((CHUNKS,)),
                pltpu.SemaphoreType.DMA((CHUNKS, 2)),
            ],
            compiler_params=pltpu.CompilerParams(collective_id=0, has_side_effects=True, vmem_limit_bytes=40 * 2**20),
        )(*[pltpu.with_memory_space_constraint(a, pltpu.HBM) for a in (velocity, jnp.asarray(gdev), jnp.asarray(floc), jnp.asarray(twid))])

    return jax.shard_map(
        step, mesh=mesh, in_specs=(P(None, None, "gy", "gz"),), out_specs=P(None, None, "gy", "gz"), check_vma=False
    )
```

```python
import jax
import jax.numpy as jnp
import ml_dtypes
import numpy as np
from jax import lax
from jax.experimental import pallas as pl
from jax.experimental.pallas import tpu as pltpu
from jax.sharding import PartitionSpec as P

MESH = pl.DeviceIdType.MESH
F32 = jnp.float32
BF16 = jnp.bfloat16
CHUNKS = 3
NZD = 8


def reversed_bits(value):
    return int(format(value, "04b")[::-1], 2)


def split_host(table):
    high = table.astype(np.float32).astype(ml_dtypes.bfloat16)
    low = (table - high.astype(np.float64)).astype(ml_dtypes.bfloat16)
    return np.stack([high, low])


def device_table():
    index = np.arange(256)
    q, z = index // NZD, index % NZD
    core, y, x = q // 16, q // 4 % 4, q % 4
    cz, cy = y % 2 * 8 + z, y // 2 * 8 + x * 2 + core
    kz = np.array([reversed_bits(c) for c in cz])
    ky = np.array([reversed_bits(c) for c in cy])
    phase = -2.0 * np.pi * ((kz[:, None] * cz[None, :] + ky[:, None] * cy[None, :]) % 16) / 16
    c, s = np.cos(phase), np.sin(phase)
    return split_host(np.block([[c, -s], [s, c]]))


def local_order():
    half, z, row = np.meshgrid(np.arange(2), np.arange(8), np.arange(16), indexing="ij")
    return (z * 32 + half * 16 + row).reshape(256)


def local_table(order):
    index = np.arange(256)
    phase = -2.0 * np.pi * ((index[:, None] * order[None, :]) % 256) / 256
    return (np.stack([np.cos(phase), np.sin(phase)]) / 64).astype(np.float32)


def twiddle_table(order):
    frequency = np.array([reversed_bits(c) for c in range(16)])
    phase = -2.0 * np.pi * ((frequency[:, None] * order[None, :]) % 4096) / 4096
    both = np.stack([np.cos(phase), np.sin(phase)], axis=1).astype(np.float32)
    return np.repeat(both[:, :, None, :], 8, axis=2)


def split(values):
    high = values.astype(BF16)
    return high, (values - high.astype(F32)).astype(BF16)


def mm(left, right):
    return jnp.dot(left, right, preferred_element_type=F32)


def transformed(tiles, ytab, ztab):
    flat = tiles.reshape(1024, 128)
    rows = [jnp.concatenate([flat[pl.ds(p * 4 + s, 128, stride=8), :] for s in range(4)], axis=1) for p in range(2)]
    xh, xl = split(jnp.concatenate(rows, axis=0))
    v = mm(xh, ztab[0]) + mm(xl, ztab[0]) + mm(xh, ztab[1])
    planes = [jnp.concatenate([v[p * 128 : p * 128 + 128, :256], v[p * 128 : p * 128 + 128, 256:]], axis=0) for p in range(2)]
    vh, vl = split(jnp.concatenate(planes, axis=1))
    return mm(ytab[0], vh) + mm(ytab[0], vl) + mm(ytab[1], vh)


def kernel(
    x_hbm, gdev_hbm, floc_hbm, twid_hbm, out, part, last, ytab, ztab,
    xin, send_p, recv_p, mid_in, mid_out, recv_q, recv_r, gdev, floc, twid,
    in_sem, const_sem, psend, precv, qsend, qrecv, bsend, brecv, rsend, rrecv,
):
    gz, gy = lax.axis_index("gz"), lax.axis_index("gy")
    yl, z = gz // 8, gz % 8
    yh, xc, co = gy // 8, gy // 2 % 4, gy % 2
    yc = yh * 2 + yl
    row = yc * 4 + xc
    q = co * 16 + row

    def z_partner(t):
        zt = (z + t) % 8
        return zt, (yl * 8 + zt, gy)

    def q_partner(t, dc):
        a, b = t // 4, t % 4
        dy, dx = a + co * (b - a), b + co * (a - b)
        y2, x2, c2 = (yc + dy) % 4, (xc + dx) % 4, (co + dc) % 2
        return y2 * 4 + x2, (y2 % 2 * 8 + z, y2 // 2 * 8 + x2 * 2 + c2)

    loads = [pltpu.make_async_copy(x_hbm.at[:, pl.ds(2 * c, 2)], xin.at[:, pl.ds(2 * c, 2)], in_sem.at[c]) for c in range(CHUNKS)]
    consts = [
        pltpu.make_async_copy(floc_hbm, floc, const_sem.at[0]),
        pltpu.make_async_copy(twid_hbm, twid, const_sem.at[1]),
        pltpu.make_async_copy(gdev_hbm, gdev, const_sem.at[2]),
    ]
    loads[0].start()

    barrier = pltpu.get_barrier_semaphore()

    @pl.loop(1, 8)
    def _(t):
        pl.semaphore_signal(barrier, inc=1, device_id=z_partner(t)[1], device_id_type=MESH)

    @pl.loop(1, 32)
    def _(t):
        pl.semaphore_signal(barrier, inc=1, device_id=q_partner(t // 2, t % 2)[1], device_id_type=MESH)

    for copy in loads[1:] + consts:
        copy.start()

    def relayout(c, half):
        flat = send_p.at[c, half].reshape(1024, 128)
        for p in range(2):
            for r in range(2):
                for h in range(2):
                    for zt in range(8):
                        first = zt * 32 + half * 16
                        flat[pl.ds(zt * 128 + p * 4 + r * 2 + h, 16, stride=8), :] = xin[r, 2 * c + p, first : first + 16, h * 128 : h * 128 + 128]

    def remote(source, target, send_sem, recv_sem, device):
        return pltpu.make_async_remote_copy(source, target, send_sem, recv_sem, device_id=device, device_id_type=MESH)

    def p_copy(c, half, t):
        zt, device = z_partner(t)
        return remote(send_p.at[c, half, zt], recv_p.at[c, half, z], psend.at[c], precv.at[c, half], device)

    def p_own(c, half):
        return pltpu.make_async_copy(send_p.at[c, half, z], recv_p.at[c, half, z], precv.at[c, half])

    def returned(c, half):
        return last if (c, half) == (CHUNKS - 1, 1) else recv_r.at[c, half]

    def r_copy(c, half, t):
        zt, device = z_partner(t)
        return remote(recv_q.at[c, half, zt], returned(c, half).at[z], rsend.at[c], rrecv.at[c, half], device)

    def r_own(c, half):
        return pltpu.make_async_copy(recv_q.at[c, half, z], returned(c, half).at[z], rrecv.at[c, half])

    def q_copy(c, t, dc):
        there, device = q_partner(t, dc)
        half = (co + dc) % 2
        return remote(recv_p.at[c, half, :, there], mid_in.at[c, q], qsend.at[c], qrecv.at[c], device)

    def q_own(c):
        return pltpu.make_async_copy(recv_p.at[c, co, :, row], mid_in.at[c, q], qrecv.at[c])

    def b_copy(c, t, dc):
        there, device = q_partner(t, dc)
        half = (co + dc) % 2
        return remote(mid_out.at[c, half * 16 + there], recv_q.at[c, co, :, row], bsend.at[c], brecv.at[c, co], device)

    def b_own(c):
        return pltpu.make_async_copy(mid_out.at[c, q], recv_q.at[c, co, :, row], brecv.at[c, co])

    def start_z(copy, own, c, half):
        own(c, half).start()

        @pl.loop(1, 8)
        def _(t):
            copy(c, half, t).start()

    def wait_bytes(ref, sem):
        pltpu.make_async_copy(ref, ref, sem).wait()

    def start_q(c, half):
        dc = (half + co) % 2

        @pl.loop(1, 8)
        def _(t):
            q_copy(c, t, dc).start()
            q_copy(c, 16 - t, dc).start()

        q_copy(c, 8, dc).start()

        @pl.when(dc == 0)
        def _():
            q_own(c).start()

        @pl.when(dc == 1)
        def _():
            q_copy(c, 0, 1).start()

    def start_b(c):
        @pl.loop(1, 8)
        def _(t):
            for dc in range(2):
                b_copy(c, t, dc).start()
                b_copy(c, 16 - t, dc).start()

        b_copy(c, 8, 0).start()
        b_copy(c, 8, 1).start()
        b_copy(c, 0, 1).start()
        b_own(c).start()

    def read_rows(ref, count):
        flat = ref.reshape(count * 8, 128)
        rows = [
            jnp.concatenate([flat[pl.ds(p * 4 + r * 2 + h, count, stride=8), :] for p in range(2) for h in range(2)], axis=1)
            for r in range(2)
        ]
        return jnp.concatenate(rows, axis=0)

    def middle(c):
        xh, xl = split(read_rows(mid_in.at[c], 256))
        y = mm(gdev[0], xh) + mm(gdev[0], xl) + mm(gdev[1], xh)
        flat = mid_out.at[c].reshape(2048, 128)
        for p in range(2):
            for r in range(2):
                for h in range(2):
                    flat[pl.ds(p * 4 + r * 2 + h, 256, stride=8), :] = y[r * 256 : r * 256 + 256, (p * 2 + h) * 128 : (p * 2 + h) * 128 + 128]

    def twisted(axis, position):
        fr, fi = floc[axis, 0], floc[axis, 1]
        tc, ts = twid[axis, position, 0, 0:1], twid[axis, position, 1, 0:1]
        return fr * tc - fi * ts, fr * ts + fi * tc

    def tables():
        a, b = twisted(0, gy)
        for half in range(2):
            ah, bh = a[:, half * 128 : half * 128 + 128], b[:, half * 128 : half * 128 + 128]
            full = jnp.concatenate([jnp.concatenate([ah, -bh], axis=1), jnp.concatenate([bh, ah], axis=1)], axis=0)
            ytab[half, 0], ytab[half, 1] = split(full)
        a, b = twisted(1, gz)
        a, b = a.T, b.T
        full = jnp.concatenate([jnp.concatenate([a, b], axis=1), jnp.concatenate([-b, a], axis=1)], axis=0)
        ztab[0], ztab[1] = split(full)

    def final_first(c):
        part[...] = transformed(recv_r.at[c, 0], ytab.at[0], ztab)

    def final_second(c):
        u = part[...] + transformed(recv_r.at[c, 1], ytab.at[1], ztab)
        for p in range(2):
            for r in range(2):
                out[r, 2 * c + p] = u[r * 256 : r * 256 + 256, p * 256 : p * 256 + 256]

    loads[0].wait()
    relayout(0, 0)
    pl.semaphore_wait(barrier, 38)
    start_z(p_copy, p_own, 0, 0)
    relayout(0, 1)
    start_z(p_copy, p_own, 0, 1)
    for c in range(1, CHUNKS):
        loads[c].wait()
        relayout(c, 0)
        relayout(c, 1)
    for copy in consts:
        copy.wait()
    tables()
    wait_bytes(recv_p.at[0, 0], precv.at[0, 0])
    start_q(0, 0)
    start_z(p_copy, p_own, 1, 0)
    wait_bytes(recv_p.at[0, 1], precv.at[0, 1])
    start_q(0, 1)
    start_z(p_copy, p_own, 1, 1)
    wait_bytes(mid_in.at[0], qrecv.at[0])
    middle(0)
    start_b(0)
    wait_bytes(recv_p.at[1, 0], precv.at[1, 0])
    start_q(1, 0)
    start_z(p_copy, p_own, 2, 0)
    wait_bytes(recv_p.at[1, 1], precv.at[1, 1])
    start_q(1, 1)
    start_z(p_copy, p_own, 2, 1)
    wait_bytes(recv_q.at[0, 0], brecv.at[0, 0])
    start_z(r_copy, r_own, 0, 0)
    wait_bytes(recv_q.at[0, 1], brecv.at[0, 1])
    start_z(r_copy, r_own, 0, 1)
    wait_bytes(mid_in.at[1], qrecv.at[1])
    middle(1)
    start_b(1)
    wait_bytes(recv_p.at[2, 0], precv.at[2, 0])
    start_q(2, 0)
    wait_bytes(recv_p.at[2, 1], precv.at[2, 1])
    start_q(2, 1)
    wait_bytes(recv_q.at[1, 0], brecv.at[1, 0])
    start_z(r_copy, r_own, 1, 0)
    wait_bytes(recv_q.at[1, 1], brecv.at[1, 1])
    start_z(r_copy, r_own, 1, 1)
    wait_bytes(mid_in.at[2], qrecv.at[2])
    middle(2)
    start_b(2)
    wait_bytes(recv_r.at[0, 0], rrecv.at[0, 0])
    final_first(0)
    wait_bytes(recv_r.at[0, 1], rrecv.at[0, 1])
    final_second(0)
    wait_bytes(recv_q.at[2, 0], brecv.at[2, 0])
    start_z(r_copy, r_own, 2, 0)
    wait_bytes(recv_q.at[2, 1], brecv.at[2, 1])
    start_z(r_copy, r_own, 2, 1)
    for c in range(CHUNKS):
        wait_bytes(send_p.at[c, :, pl.ds(0, 7)], psend.at[c])
        wait_bytes(mid_in.at[c, pl.ds(0, 31)], qsend.at[c])
    wait_bytes(recv_r.at[1, 0], rrecv.at[1, 0])
    final_first(1)
    for c in range(CHUNKS):
        wait_bytes(mid_out.at[c, pl.ds(0, 31)], bsend.at[c])
    wait_bytes(recv_r.at[1, 1], rrecv.at[1, 1])
    final_second(1)
    wait_bytes(recv_r.at[0, :, pl.ds(0, 7)], rsend.at[0])
    wait_bytes(recv_r.at[1, :, pl.ds(0, 7)], rsend.at[1])
    wait_bytes(recv_r.at[2, 0], rrecv.at[2, 0])
    final_first(2)
    wait_bytes(last, rrecv.at[2, 1])
    wait_bytes(recv_r.at[2, :, pl.ds(0, 7)], rsend.at[2])


def finish_kernel(done, part, last, ytab, ztab, o_hbm, rest, sems):
    early = [pltpu.make_async_copy(done.at[r, a], o_hbm.at[r, a], sems.at[r, a]) for r in range(2) for a in range(4)]
    for copy in early:
        copy.start()
    u = part[...] + transformed(last, ytab.at[1], ztab)
    late = []
    for p in range(2):
        for r in range(2):
            rest[r, p] = u[r * 256 : r * 256 + 256, p * 256 : p * 256 + 256]
            copy = pltpu.make_async_copy(rest.at[r, p], o_hbm.at[r, 4 + p], sems.at[r, 4 + p])
            copy.start()
            late.append(copy)
    for copy in early + late:
        copy.wait()


def solution(mesh):
    gdev = device_table()
    orders = (local_order(), np.arange(256))
    floc = np.stack([local_table(order) for order in orders])
    twid = np.stack([twiddle_table(order) for order in orders])

    def step(velocity):
        anywhere = pl.BlockSpec(memory_space=pl.ANY)
        halves = pltpu.VMEM((CHUNKS, 2, 8, 16, 8, 128), F32)
        middles = pltpu.VMEM((CHUNKS, 32, 8, 8, 128), F32)
        inside = pl.BlockSpec(memory_space=pltpu.VMEM)
        held = pl.pallas_call(
            kernel,
            out_shape=[
                pltpu.VMEM((2, 4, 256, 256), F32),
                pltpu.VMEM((512, 512), F32),
                pltpu.VMEM((8, 16, 8, 128), F32),
                pltpu.VMEM((2, 2, 512, 256), BF16),
                pltpu.VMEM((2, 512, 512), BF16),
            ],
            in_specs=[pl.BlockSpec(memory_space=pltpu.HBM)] * 4,
            out_specs=[inside] * 5,
            scratch_shapes=[
                pltpu.VMEM((2, 6, 256, 256), F32),
                halves,
                halves,
                middles,
                middles,
                halves,
                halves,
                pltpu.VMEM((2, 512, 512), BF16),
                pltpu.VMEM((2, 2, 256, 256), F32),
                pltpu.VMEM((2, 16, 2, 8, 256), F32),
                pltpu.SemaphoreType.DMA((CHUNKS,)),
                pltpu.SemaphoreType.DMA((3,)),
                pltpu.SemaphoreType.DMA((CHUNKS,)),
                pltpu.SemaphoreType.DMA((CHUNKS, 2)),
                pltpu.SemaphoreType.DMA((CHUNKS,)),
                pltpu.SemaphoreType.DMA((CHUNKS,)),
                pltpu.SemaphoreType.DMA((CHUNKS,)),
                pltpu.SemaphoreType.DMA((CHUNKS, 2)),
                pltpu.SemaphoreType.DMA((CHUNKS,)),
                pltpu.SemaphoreType.DMA((CHUNKS, 2)),
            ],
            compiler_params=pltpu.CompilerParams(collective_id=0, has_side_effects=True, vmem_limit_bytes=40 * 2**20),
        )(*[pltpu.with_memory_space_constraint(a, pltpu.HBM) for a in (velocity, jnp.asarray(gdev), jnp.asarray(floc), jnp.asarray(twid))])
        return pl.pallas_call(
            finish_kernel,
            out_shape=jax.ShapeDtypeStruct(velocity.shape, F32),
            in_specs=[inside] * 5,
            out_specs=anywhere,
            scratch_shapes=[pltpu.VMEM((2, 2, 256, 256), F32), pltpu.SemaphoreType.DMA((2, 6))],
            compiler_params=pltpu.CompilerParams(vmem_limit_bytes=16 * 2**20),
        )(*[pltpu.with_memory_space_constraint(a, pltpu.VMEM) for a in held])

    return jax.shard_map(
        step, mesh=mesh, in_specs=(P(None, None, "gy", "gz"),), out_specs=P(None, None, "gy", "gz"), check_vma=False
    )
```

```python
import jax
import jax.numpy as jnp
import ml_dtypes
import numpy as np
from jax import lax
from jax.experimental import pallas as pl
from jax.experimental.pallas import tpu as pltpu
from jax.sharding import PartitionSpec as P

MESH = pl.DeviceIdType.MESH
F32 = jnp.float32
BF16 = jnp.bfloat16
CHUNKS = 3
NZD = 8


def reversed_bits(value):
    return int(format(value, "04b")[::-1], 2)


def split_host(table):
    high = table.astype(np.float32).astype(ml_dtypes.bfloat16)
    low = (table - high.astype(np.float64)).astype(ml_dtypes.bfloat16)
    return np.stack([high, low])


def device_table():
    index = np.arange(256)
    q, z = index // NZD, index % NZD
    core, y, x = q // 16, q // 4 % 4, q % 4
    cz, cy = y % 2 * 8 + z, y // 2 * 8 + x * 2 + core
    kz = np.array([reversed_bits(c) for c in cz])
    ky = np.array([reversed_bits(c) for c in cy])
    phase = -2.0 * np.pi * ((kz[:, None] * cz[None, :] + ky[:, None] * cy[None, :]) % 16) / 16
    c, s = np.cos(phase), np.sin(phase)
    return split_host(np.block([[c, -s], [s, c]]))


def local_order():
    half, z, row = np.meshgrid(np.arange(2), np.arange(8), np.arange(16), indexing="ij")
    return (z * 32 + half * 16 + row).reshape(256)


def local_table(order):
    index = np.arange(256)
    phase = -2.0 * np.pi * ((index[:, None] * order[None, :]) % 256) / 256
    return (np.stack([np.cos(phase), np.sin(phase)]) / 64).astype(np.float32)


def twiddle_table(order):
    frequency = np.array([reversed_bits(c) for c in range(16)])
    phase = -2.0 * np.pi * ((frequency[:, None] * order[None, :]) % 4096) / 4096
    both = np.stack([np.cos(phase), np.sin(phase)], axis=1).astype(np.float32)
    return np.repeat(both[:, :, None, :], 8, axis=2)


def split(values):
    high = values.astype(BF16)
    return high, (values - high.astype(F32)).astype(BF16)


def mm(left, right):
    return jnp.dot(left, right, preferred_element_type=F32)


def z_transformed(tiles, ztab):
    flat = tiles.reshape(1024, 128)
    rows = [jnp.concatenate([flat[pl.ds(p * 4 + s, 128, stride=8), :] for s in range(4)], axis=1) for p in range(2)]
    xh, xl = split(jnp.concatenate(rows, axis=0))
    v = mm(xh, ztab[0]) + mm(xl, ztab[0]) + mm(xh, ztab[1])
    return [jnp.concatenate([v[p * 128 : p * 128 + 128, :256], v[p * 128 : p * 128 + 128, 256:]], axis=0) for p in range(2)]


def y_sum(v, ytab):
    vh, vl = split(v)
    return mm(ytab[0], vh) + mm(ytab[0], vl) + mm(ytab[1], vh)


def kernel(
    x_hbm, gdev_hbm, floc_hbm, twid_hbm, out, part, last, ytab, ztab,
    xin, send_p, recv_p, mid_in, mid_out, recv_q, recv_r, gdev, floc, twid,
    in_sem, const_sem, psend, precv, qsend, qrecv, bsend, brecv, rsend, rrecv,
):
    gz, gy = lax.axis_index("gz"), lax.axis_index("gy")
    yl, z = gz // 8, gz % 8
    yh, xc, co = gy // 8, gy // 2 % 4, gy % 2
    yc = yh * 2 + yl
    row = yc * 4 + xc
    q = co * 16 + row

    def z_partner(t):
        zt = (z + t) % 8
        return zt, (yl * 8 + zt, gy)

    def q_partner(t, dc):
        a, b = t // 4, t % 4
        dy, dx = a + co * (b - a), b + co * (a - b)
        y2, x2, c2 = (yc + dy) % 4, (xc + dx) % 4, (co + dc) % 2
        return y2 * 4 + x2, (y2 % 2 * 8 + z, y2 // 2 * 8 + x2 * 2 + c2)

    loads = [pltpu.make_async_copy(x_hbm.at[:, pl.ds(2 * c, 2)], xin.at[:, pl.ds(2 * c, 2)], in_sem.at[c]) for c in range(CHUNKS)]
    consts = [
        pltpu.make_async_copy(floc_hbm, floc, const_sem.at[0]),
        pltpu.make_async_copy(twid_hbm, twid, const_sem.at[1]),
        pltpu.make_async_copy(gdev_hbm, gdev, const_sem.at[2]),
    ]
    loads[0].start()

    barrier = pltpu.get_barrier_semaphore()

    @pl.loop(1, 8)
    def _(t):
        pl.semaphore_signal(barrier, inc=1, device_id=z_partner(t)[1], device_id_type=MESH)

    @pl.loop(1, 32)
    def _(t):
        pl.semaphore_signal(barrier, inc=1, device_id=q_partner(t // 2, t % 2)[1], device_id_type=MESH)

    for copy in loads[1:] + consts:
        copy.start()

    def relayout(c, half):
        flat = send_p.at[c, half].reshape(1024, 128)
        for p in range(2):
            for r in range(2):
                for h in range(2):
                    for zt in range(8):
                        first = zt * 32 + half * 16
                        flat[pl.ds(zt * 128 + p * 4 + r * 2 + h, 16, stride=8), :] = xin[r, 2 * c + p, first : first + 16, h * 128 : h * 128 + 128]

    def remote(source, target, send_sem, recv_sem, device):
        return pltpu.make_async_remote_copy(source, target, send_sem, recv_sem, device_id=device, device_id_type=MESH)

    def p_copy(c, half, t):
        zt, device = z_partner(t)
        return remote(send_p.at[c, half, zt], recv_p.at[c, half, z], psend.at[c], precv.at[c, half], device)

    def p_own(c, half):
        return pltpu.make_async_copy(send_p.at[c, half, z], recv_p.at[c, half, z], precv.at[c, half])

    def returned(c, half):
        return last if (c, half) == (CHUNKS - 1, 1) else recv_r.at[c, half]

    def r_copy(c, half, t):
        zt, device = z_partner(t)
        return remote(recv_q.at[c, half, zt], returned(c, half).at[z], rsend.at[c], rrecv.at[c, half], device)

    def r_own(c, half):
        return pltpu.make_async_copy(recv_q.at[c, half, z], returned(c, half).at[z], rrecv.at[c, half])

    def q_copy(c, t, dc):
        there, device = q_partner(t, dc)
        half = (co + dc) % 2
        return remote(recv_p.at[c, half, :, there], mid_in.at[c, q], qsend.at[c], qrecv.at[c], device)

    def q_own(c):
        return pltpu.make_async_copy(recv_p.at[c, co, :, row], mid_in.at[c, q], qrecv.at[c])

    def b_copy(c, t, dc):
        there, device = q_partner(t, dc)
        half = (co + dc) % 2
        return remote(mid_out.at[c, half * 16 + there], recv_q.at[c, co, :, row], bsend.at[c], brecv.at[c, co], device)

    def b_own(c):
        return pltpu.make_async_copy(mid_out.at[c, q], recv_q.at[c, co, :, row], brecv.at[c, co])

    def start_z(copy, own, c, half):
        own(c, half).start()

        @pl.loop(1, 8)
        def _(t):
            copy(c, half, t).start()

    def wait_bytes(ref, sem):
        pltpu.make_async_copy(ref, ref, sem).wait()

    def start_q(c, half):
        dc = (half + co) % 2

        @pl.loop(1, 8)
        def _(t):
            q_copy(c, t, dc).start()
            q_copy(c, 16 - t, dc).start()

        q_copy(c, 8, dc).start()

        @pl.when(dc == 0)
        def _():
            q_own(c).start()

        @pl.when(dc == 1)
        def _():
            q_copy(c, 0, 1).start()

    def start_b(c):
        @pl.loop(1, 8)
        def _(t):
            for dc in range(2):
                b_copy(c, t, dc).start()
                b_copy(c, 16 - t, dc).start()

        b_copy(c, 8, 0).start()
        b_copy(c, 8, 1).start()
        b_copy(c, 0, 1).start()
        b_own(c).start()

    def read_rows(ref, count):
        flat = ref.reshape(count * 8, 128)
        rows = [
            jnp.concatenate([flat[pl.ds(p * 4 + r * 2 + h, count, stride=8), :] for p in range(2) for h in range(2)], axis=1)
            for r in range(2)
        ]
        return jnp.concatenate(rows, axis=0)

    def middle(c):
        xh, xl = split(read_rows(mid_in.at[c], 256))
        y = mm(gdev[0], xh) + mm(gdev[0], xl) + mm(gdev[1], xh)
        flat = mid_out.at[c].reshape(2048, 128)
        for p in range(2):
            for r in range(2):
                for h in range(2):
                    flat[pl.ds(p * 4 + r * 2 + h, 256, stride=8), :] = y[r * 256 : r * 256 + 256, (p * 2 + h) * 128 : (p * 2 + h) * 128 + 128]

    def twisted(axis, position):
        fr, fi = floc[axis, 0], floc[axis, 1]
        tc, ts = twid[axis, position, 0, 0:1], twid[axis, position, 1, 0:1]
        return fr * tc - fi * ts, fr * ts + fi * tc

    def tables():
        a, b = twisted(0, gy)
        for half in range(2):
            ah, bh = a[:, half * 128 : half * 128 + 128], b[:, half * 128 : half * 128 + 128]
            full = jnp.concatenate([jnp.concatenate([ah, -bh], axis=1), jnp.concatenate([bh, ah], axis=1)], axis=0)
            ytab[half, 0], ytab[half, 1] = split(full)
        a, b = twisted(1, gz)
        a, b = a.T, b.T
        full = jnp.concatenate([jnp.concatenate([a, b], axis=1), jnp.concatenate([-b, a], axis=1)], axis=0)
        ztab[0], ztab[1] = split(full)

    def final_first(c):
        part[...] = y_sum(jnp.concatenate(z_transformed(recv_r.at[c, 0], ztab), axis=1), ytab[0])

    def final_second(c):
        u = part[...] + y_sum(jnp.concatenate(z_transformed(recv_r.at[c, 1], ztab), axis=1), ytab[1])
        for p in range(2):
            for r in range(2):
                out[r, 2 * c + p] = u[r * 256 : r * 256 + 256, p * 256 : p * 256 + 256]

    loads[0].wait()
    relayout(0, 0)
    pl.semaphore_wait(barrier, 38)
    start_z(p_copy, p_own, 0, 0)
    relayout(0, 1)
    start_z(p_copy, p_own, 0, 1)
    for c in range(1, CHUNKS):
        loads[c].wait()
        relayout(c, 0)
        relayout(c, 1)
        if c == 1:
            start_z(p_copy, p_own, 1, 0)
            start_z(p_copy, p_own, 1, 1)
    for copy in consts:
        copy.wait()
    tables()
    wait_bytes(recv_p.at[0, 0], precv.at[0, 0])
    start_q(0, 0)
    start_z(p_copy, p_own, 2, 0)
    wait_bytes(recv_p.at[0, 1], precv.at[0, 1])
    start_q(0, 1)
    start_z(p_copy, p_own, 2, 1)
    wait_bytes(mid_in.at[0], qrecv.at[0])
    middle(0)
    start_b(0)
    wait_bytes(recv_p.at[1, 0], precv.at[1, 0])
    start_q(1, 0)
    wait_bytes(recv_p.at[1, 1], precv.at[1, 1])
    start_q(1, 1)
    wait_bytes(recv_q.at[0, 0], brecv.at[0, 0])
    start_z(r_copy, r_own, 0, 0)
    wait_bytes(recv_q.at[0, 1], brecv.at[0, 1])
    start_z(r_copy, r_own, 0, 1)
    wait_bytes(mid_in.at[1], qrecv.at[1])
    middle(1)
    start_b(1)
    wait_bytes(recv_p.at[2, 0], precv.at[2, 0])
    start_q(2, 0)
    wait_bytes(recv_p.at[2, 1], precv.at[2, 1])
    start_q(2, 1)
    wait_bytes(recv_q.at[1, 0], brecv.at[1, 0])
    start_z(r_copy, r_own, 1, 0)
    wait_bytes(recv_q.at[1, 1], brecv.at[1, 1])
    start_z(r_copy, r_own, 1, 1)
    wait_bytes(mid_in.at[2], qrecv.at[2])
    middle(2)
    start_b(2)
    wait_bytes(recv_r.at[0, 0], rrecv.at[0, 0])
    final_first(0)
    wait_bytes(recv_r.at[0, 1], rrecv.at[0, 1])
    final_second(0)
    wait_bytes(recv_q.at[2, 0], brecv.at[2, 0])
    start_z(r_copy, r_own, 2, 0)
    wait_bytes(recv_q.at[2, 1], brecv.at[2, 1])
    start_z(r_copy, r_own, 2, 1)
    for c in range(CHUNKS):
        wait_bytes(send_p.at[c, :, pl.ds(0, 7)], psend.at[c])
        wait_bytes(mid_in.at[c, pl.ds(0, 31)], qsend.at[c])
    wait_bytes(recv_r.at[1, 0], rrecv.at[1, 0])
    final_first(1)
    for c in range(CHUNKS):
        wait_bytes(mid_out.at[c, pl.ds(0, 31)], bsend.at[c])
    wait_bytes(recv_r.at[1, 1], rrecv.at[1, 1])
    final_second(1)
    wait_bytes(recv_r.at[0, :, pl.ds(0, 7)], rsend.at[0])
    wait_bytes(recv_r.at[1, :, pl.ds(0, 7)], rsend.at[1])
    wait_bytes(recv_r.at[2, 0], rrecv.at[2, 0])
    final_first(2)
    wait_bytes(last, rrecv.at[2, 1])
    wait_bytes(recv_r.at[2, :, pl.ds(0, 7)], rsend.at[2])


def finish_kernel(done, part, last, ytab, ztab, o_hbm, rest, sems):
    early = [pltpu.make_async_copy(done.at[r, a], o_hbm.at[r, a], sems.at[r, a]) for r in range(2) for a in range(4)]
    for copy in early:
        copy.start()
    late = []
    for p, v in enumerate(z_transformed(last, ztab)):
        u = part[:, p * 256 : p * 256 + 256] + y_sum(v, ytab[1])
        for r in range(2):
            rest[r, p] = u[r * 256 : r * 256 + 256]
            copy = pltpu.make_async_copy(rest.at[r, p], o_hbm.at[r, 4 + p], sems.at[r, 4 + p])
            copy.start()
            late.append(copy)
    for copy in early + late:
        copy.wait()


def solution(mesh):
    gdev = device_table()
    orders = (local_order(), np.arange(256))
    floc = np.stack([local_table(order) for order in orders])
    twid = np.stack([twiddle_table(order) for order in orders])

    def step(velocity):
        anywhere = pl.BlockSpec(memory_space=pl.ANY)
        halves = pltpu.VMEM((CHUNKS, 2, 8, 16, 8, 128), F32)
        middles = pltpu.VMEM((CHUNKS, 32, 8, 8, 128), F32)
        inside = pl.BlockSpec(memory_space=pltpu.VMEM)
        held = pl.pallas_call(
            kernel,
            out_shape=[
                pltpu.VMEM((2, 4, 256, 256), F32),
                pltpu.VMEM((512, 512), F32),
                pltpu.VMEM((8, 16, 8, 128), F32),
                pltpu.VMEM((2, 2, 512, 256), BF16),
                pltpu.VMEM((2, 512, 512), BF16),
            ],
            in_specs=[pl.BlockSpec(memory_space=pltpu.HBM)] * 4,
            out_specs=[inside] * 5,
            scratch_shapes=[
                pltpu.VMEM((2, 6, 256, 256), F32),
                halves,
                halves,
                middles,
                middles,
                halves,
                halves,
                pltpu.VMEM((2, 512, 512), BF16),
                pltpu.VMEM((2, 2, 256, 256), F32),
                pltpu.VMEM((2, 16, 2, 8, 256), F32),
                pltpu.SemaphoreType.DMA((CHUNKS,)),
                pltpu.SemaphoreType.DMA((3,)),
                pltpu.SemaphoreType.DMA((CHUNKS,)),
                pltpu.SemaphoreType.DMA((CHUNKS, 2)),
                pltpu.SemaphoreType.DMA((CHUNKS,)),
                pltpu.SemaphoreType.DMA((CHUNKS,)),
                pltpu.SemaphoreType.DMA((CHUNKS,)),
                pltpu.SemaphoreType.DMA((CHUNKS, 2)),
                pltpu.SemaphoreType.DMA((CHUNKS,)),
                pltpu.SemaphoreType.DMA((CHUNKS, 2)),
            ],
            compiler_params=pltpu.CompilerParams(collective_id=0, has_side_effects=True, vmem_limit_bytes=40 * 2**20),
        )(*[pltpu.with_memory_space_constraint(a, pltpu.HBM) for a in (velocity, jnp.asarray(gdev), jnp.asarray(floc), jnp.asarray(twid))])
        return pl.pallas_call(
            finish_kernel,
            out_shape=jax.ShapeDtypeStruct(velocity.shape, F32),
            in_specs=[inside] * 5,
            out_specs=anywhere,
            scratch_shapes=[pltpu.VMEM((2, 2, 256, 256), F32), pltpu.SemaphoreType.DMA((2, 6))],
            compiler_params=pltpu.CompilerParams(vmem_limit_bytes=16 * 2**20),
        )(*[pltpu.with_memory_space_constraint(a, pltpu.VMEM) for a in held])

    return jax.shard_map(
        step, mesh=mesh, in_specs=(P(None, None, "gy", "gz"),), out_specs=P(None, None, "gy", "gz"), check_vma=False
    )
```
